1024 devices in a mesh: expert: 64 (over z_lo, y), dp: 16 (over x, z_hi, core).
Axes of the slice: x: 4, y: 4, z: 32 (z_hi: 2, z_lo: 16; z = z_hi * 16 + z_lo), core: 2. Of those that a mesh axis runs over, the one named last changes fastest.
Arguments:
- tokens_in: bfloat16 [8192, 7168], P('expert', 'dp'), may hold values from -1.5 to 1.5
- grad_out: bfloat16 [8192, 7168], P('expert', 'dp'), may hold values from -1.5 to 1.5
- routes: int32 [8192, 2], P('expert'), may hold values from 0 to 31, all different within a row; in each aligned block of 128 rows (0 to 127, 128 to 255, ...) at most 12 rows name the same one
- gate_probs: float32 [8192, 2], P('expert'), may hold values from 0.1 to 1
- saved_gate: bfloat16 [64, 768, 512], P('expert'), may hold values from -6 to 6
- saved_up: bfloat16 [64, 768, 512], P('expert'), may hold values from -6 to 6
- w_gate: bfloat16 [64, 7168, 512], P('expert', 'dp'), may hold values from -0.25 to 0.25
- w_up: bfloat16 [64, 7168, 512], P('expert', 'dp'), may hold values from -0.25 to 0.25
- w_down: bfloat16 [64, 512, 7168], P('expert', None, 'dp'), may hold values from -0.0625 to 0.0625
Outputs:
- grad_tokens: bfloat16 [8192, 7168], P('expert', 'dp')
- grad_w_gate: bfloat16 [64, 7168, 512], P('expert', 'dp')
- grad_w_up: bfloat16 [64, 7168, 512], P('expert', 'dp')
- grad_w_down: bfloat16 [64, 512, 7168], P('expert', None, 'dp')
The draws below stay inside these ranges and needn't reach their ends.
Inputs may be any that keep to these rules, and one draw needn't show every extreme that they name: `routes`: each row names 2 different experts. Within the 128 rows of one index of the expert axis no expert is named more than 12 times, and in some such block one expert is named exactly 12 times.
All inputs are finite; a program needn't handle non-finite values.
Results may differ from the reference program's by a relative error of at most 0.0072.
Values may be sent and summed in bfloat16 or wider, within the bound.
A program may use at most 32 MiB of HBM per device.

```python
import math
import jax
import jax.numpy as jnp
import numpy as np
from jax import lax

D = 7168
K = 2
TOK_DEV = 128
HALF_HIDDEN = 512
EXPERTS = 32
BLOCKS = 64
CAPACITY = 12
ROWS = 768
TOKENS = 8192
N_EXPERT = 64


def block_scale(rng, dims, cuts, low, high):
    gain = 1.0
    for axis_at, shards_of in cuts:
        heights = jax.random.uniform(jax.random.fold_in(jax.random.fold_in(rng, 6), axis_at), (shards_of,), jnp.float32, low / len(cuts), high / len(cuts))
        gain = gain * jnp.repeat(jnp.exp(heights), dims[axis_at] // shards_of).reshape((-1,) + (1,) * (len(dims) - 1 - axis_at))
    return gain


def shared_out(own_key, own, number, rows, number_of, top, reach, slope):
    ranking = jax.random.permutation(own_key, number_of)
    packed, common = load_shares(number_of, rows * top, reach, slope, True), load_shares(number_of, rows * top, reach, slope, False)
    places = jnp.arange(number_of)

    def named(lengths, turn):
        used = int((lengths > 0).sum())
        fixed = max(1, used // 4)
        moved = fixed + (places - fixed + turn * (used - fixed)) % max(1, number_of - fixed)
        return jnp.zeros((number_of,), jnp.int32).at[ranking[jnp.where(places < fixed, places, moved)]].set(jnp.asarray(lengths, jnp.int32))

    lengths = jnp.where(number % 4 == 0, named(packed, number // 4), named(common, number - number // 4 - 1))
    mixed = jax.random.permutation(jax.random.fold_in(own, 3), number_of)
    source_of, sink = mixed[0:number_of // 2 * 2:2], mixed[1:number_of // 2 * 2:2]
    slack = jnp.minimum(lengths[source_of] - 1, reach - lengths[sink]) // 2
    slack = jnp.where((source_of == ranking[0]) | (sink == ranking[0]) | (lengths[sink] == 0), 0, jnp.maximum(slack, 0))
    moved = jax.random.randint(jax.random.fold_in(own, 4), (number_of // 2,), 0, 1 << 20) % (slack + 1)
    lengths = lengths.at[source_of].add(-moved).at[sink].add(moved)
    members = jnp.searchsorted(jnp.cumsum(lengths), jnp.arange(rows * top), side="right").astype(jnp.int32)
    listing = members.reshape(top, rows).T
    listing = listing[jax.random.permutation(jax.random.fold_in(own, 1), rows)]
    turn = jax.random.randint(jax.random.fold_in(own, 2), (rows, 1), 0, top)
    return jnp.take_along_axis(listing, (jnp.arange(top)[None, :] + turn) % top, axis=1)


def load_shares(amount, total, limit, slope, full):
    portions = [(1 << 20) // math.isqrt(grade ** slope) + 1 for grade in range(1, amount + 1)]
    largest = limit if full else min(limit, max(-(-total // amount), total * portions[0] // sum(portions)))
    least = 1 if total - largest >= amount - 1 else 0
    given, surplus = [largest] + [least] * (amount - 1), total - largest - least * (amount - 1)
    while surplus > 0:
        free = [i for i in range(1, amount) if given[i] < largest] or [i for i in range(1, amount) if given[i] < limit]
        whole, left = sum([portions[i] for i in free]), surplus
        for i in free:
            more = min(limit - given[i], max(1, left * portions[i] // whole), surplus)
            given[i] = given[i] + more
            surplus = surplus - more
    return np.array(given)


def noise(stream_key, shape, scale, limit, pieces=(), held_as=jnp.bfloat16):
    array = jax.random.normal(stream_key, shape, jnp.float32) * scale
    if len(pieces) > 0:
        array = block_scale(stream_key, shape, pieces, -0.22, 0.18) * array
    return jnp.clip(array, min=-limit, max=limit).astype(held_as)


def setup_inputs(seed: int = 0) -> dict:
    keys = jax.random.split(jax.random.key(seed), 10)
    tokens_in = noise(keys[0], (TOKENS, D), 0.25, 1.5, ((0, 64), (1, 16)))
    grad_out = noise(keys[1], (TOKENS, D), 0.25, 1.5, ((0, 64), (1, 16)))
    routes_keys = jax.random.split(jax.random.fold_in(keys[2], 1), TOKENS // TOK_DEV)
    routes_turns = jax.random.permutation(jax.random.fold_in(keys[2], 3), TOKENS // TOK_DEV)
    routes = jax.vmap(lambda own, number: shared_out(jax.random.fold_in(keys[2], 2), own, number, TOK_DEV, EXPERTS, K, CAPACITY, 2))(routes_keys, routes_turns).reshape((TOKENS, K))
    gate_probs = jnp.clip(0.1 + 0.9 * jax.random.uniform(keys[3], (TOKENS, K), jnp.float32) ** block_scale(keys[3], (TOKENS, K), ((0, 64),), -0.2, 0.2), 0.1, 1.0)
    saved_gate = noise(keys[4], (BLOCKS, ROWS, HALF_HIDDEN), 1.0, 6.0, ((0, 64),))
    saved_up = noise(keys[5], (BLOCKS, ROWS, HALF_HIDDEN), 1.0, 6.0, ((0, 64),))
    w_gate = noise(keys[6], (BLOCKS, D, HALF_HIDDEN), HALF_HIDDEN ** -0.5, 0.25, ((0, 64), (1, 16)))
    w_up = noise(keys[7], (BLOCKS, D, HALF_HIDDEN), HALF_HIDDEN ** -0.5, 0.25, ((0, 64), (1, 16)))
    w_down = noise(keys[8], (BLOCKS, HALF_HIDDEN, D), D ** -0.5, 0.0625, ((0, 64), (2, 16)))
    return {"tokens_in": tokens_in, "grad_out": grad_out, "routes": routes, "gate_probs": gate_probs, "saved_gate": saved_gate, "saved_up": saved_up, "w_gate": w_gate, "w_up": w_up, "w_down": w_down}


def positions(routes):
    flat_routes = routes.reshape(N_EXPERT, TOK_DEV * K)
    one_hot = (flat_routes[:, :, None] == jnp.arange(EXPERTS, dtype=jnp.int32)[None, None, :]).astype(jnp.int32)
    before = jnp.cumsum(one_hot, axis=1) - one_hot
    slot_index = jnp.sum(before * one_hot, axis=2)
    source = jnp.arange(N_EXPERT, dtype=jnp.int32)[:, None]
    return (source * CAPACITY + slot_index).reshape(-1).astype(jnp.int32)


def block_backward(rows_in, rows_grad, gate_pre, up_pre, weight_gate, weight_up, weight_down):
    back_hidden = jnp.dot(rows_grad, weight_down.T, preferred_element_type=jnp.float32)
    gate_value = gate_pre.astype(jnp.float32)
    up_value = up_pre.astype(jnp.float32)
    sigma = jax.nn.sigmoid(gate_value)
    gate_grad = (back_hidden * up_value * sigma * (1.0 + gate_value * (1.0 - sigma))).astype(jnp.bfloat16)
    up_grad = (back_hidden * gate_value * sigma).astype(jnp.bfloat16)
    activation = (gate_value * sigma * up_value).astype(jnp.bfloat16)
    grad_down = jnp.dot(activation.T, rows_grad, preferred_element_type=jnp.float32).astype(jnp.bfloat16)
    grad_gate = jnp.dot(rows_in.T, gate_grad, preferred_element_type=jnp.float32).astype(jnp.bfloat16)
    grad_up = jnp.dot(rows_in.T, up_grad, preferred_element_type=jnp.float32).astype(jnp.bfloat16)
    input_grad = (jnp.dot(gate_grad, weight_gate.T, preferred_element_type=jnp.float32)
                  + jnp.dot(up_grad, weight_up.T, preferred_element_type=jnp.float32)).astype(jnp.bfloat16)
    return grad_gate, grad_up, grad_down, input_grad


def reference(tokens_in, grad_out, routes, gate_probs, saved_gate, saved_up, w_gate, w_up, w_down):
    position = positions(routes)
    flat_expert = routes.reshape(-1)
    scaled = (gate_probs[:, :, None] * grad_out[:, None, :].astype(jnp.float32)).astype(jnp.bfloat16)
    scaled = scaled.reshape(TOKENS * K, D)
    repeated = jnp.repeat(tokens_in, K, axis=0)

    def step(carry, expert):
        chosen = flat_expert == expert
        target = jnp.where(chosen, position, ROWS).astype(jnp.int32)
        rows_in = jnp.zeros((ROWS, D), jnp.bfloat16).at[target].set(repeated, mode="drop")
        rows_grad = jnp.zeros((ROWS, D), jnp.bfloat16).at[target].set(scaled, mode="drop")
        results = []
        pair = jnp.zeros((ROWS, D), jnp.float32)
        for half in range(2):
            block = 2 * expert + half
            outcome = block_backward(rows_in, rows_grad, saved_gate[block], saved_up[block],
                                     w_gate[block], w_up[block], w_down[block])
            pair = pair + outcome[3].astype(jnp.float32)
            results.append(outcome[:3])
        pair_grad = pair.astype(jnp.bfloat16)
        picked = pair_grad[jnp.minimum(position, ROWS - 1)].astype(jnp.float32)
        carry = carry + jnp.where(chosen[:, None], picked, jnp.float32(0.0))
        stacked = (jnp.stack([results[0][0], results[1][0]]),
                   jnp.stack([results[0][1], results[1][1]]),
                   jnp.stack([results[0][2], results[1][2]]))
        return carry, stacked

    start = jnp.zeros((TOKENS * K, D), jnp.float32)
    total, grads = lax.scan(step, start, jnp.arange(EXPERTS, dtype=jnp.int32))
    grad_tokens = jnp.sum(total.reshape(TOKENS, K, D), axis=1).astype(jnp.bfloat16)
    grad_w_gate = grads[0].reshape(BLOCKS, D, HALF_HIDDEN)
    grad_w_up = grads[1].reshape(BLOCKS, D, HALF_HIDDEN)
    grad_w_down = grads[2].reshape(BLOCKS, HALF_HIDDEN, D)
    return grad_tokens, grad_w_gate, grad_w_up, grad_w_down
```

```python
import functools

import jax
import jax.numpy as jnp
from jax import lax
from jax.experimental import pallas as pl
from jax.experimental.pallas import tpu as pltpu
from jax.sharding import PartitionSpec as P

MESH = pl.DeviceIdType.MESH
Y = 4
CHUNKS = 4
BF = jnp.bfloat16
F32 = jnp.float32


def dot_nn(a, b):
    return lax.dot_general(a, b, (((1,), (0,)), ((), ())), preferred_element_type=F32)


def dot_nt(a, b):
    return lax.dot_general(a, b, (((1,), (1,)), ((), ())), preferred_element_type=F32)


def dot_tn(a, b):
    return lax.dot_general(a, b, (((0,), (0,)), ((), ())), preferred_element_type=F32)


def kernel(
    cfg,
    tok_t, grad_t, routes_t, probs_t, s_gate, s_up, w_gate, w_up, w_down_t,
    o_tok, o_gate, o_up, o_down,
    meta, r_tok, r_grad, r_meta, pack_b,
    sb1, sb2, x1, x2, wd, act,
    p32, pb, ra, q32, qb, rx, w32, wb, rz, hid,
    gg, ug, bg, rp, ps, rr, ot, ro,
    sem_ys, sem_yr, sem_z1s, sem_z1r, sem_f1s, sem_f1r, sem_z2s, sem_z2r, sem_f2s, sem_f2r,
    sem_as, sem_ar, sem_xs, sem_xr, sem_hs, sem_hr, sem_gs, sem_gr, sem_cs, sem_cr,
    sem_ps, sem_pr, sem_rs, sem_rr, sem_os, sem_or,
):
    nz, nx, nzh, cap, C = cfg
    G = nz // C
    feats, toks = tok_t.shape
    hidden = s_gate.shape[2]
    w1 = sb1.shape[2]
    msg = 2 * cap
    units = 2 * nx
    rows = 2 * G * msg

    e = lax.axis_index("expert")
    d = lax.axis_index("dp")
    y, z = e % Y, e // Y
    core, zh, x = d % 2, (d // 2) % nzh, d // (2 * nzh)
    par, h = y // 2, y % 2
    zq, zr = z // G, z % G
    pair = z * Y + (y + 1 - 2 * h)
    core_to = (x * nzh + zh) * 2 + (1 - core)
    zh_to = (x * nzh + (1 - zh)) * 2 + core

    def x_to(j):
        return (((x + j) % nx) * nzh + zh) * 2 + core

    def send_z(c, j):
        return ((zq + c) % C) * G + (zr + j) % G

    def recv_z(c, j):
        return ((zq + C - c) % C) * G + (zr + G - j) % G

    def group(c):
        return (zq + C - c) % C

    def remote(src, dst, ss, rs, ee, dd):
        return pltpu.make_async_remote_copy(
            src_ref=src, dst_ref=dst, send_sem=ss, recv_sem=rs,
            device_id=(ee, dd), device_id_type=MESH,
        )

    def loop(lo, hi, body):
        if hi - lo == 1:
            body(lo)
        elif hi > lo:
            lax.fori_loop(lo, hi, lambda i, _: (body(i), 0)[1], 0)

    barrier = pltpu.get_barrier_semaphore()

    def greet(ee, dd):
        pl.semaphore_signal(barrier, inc=1, device_id=(ee, dd), device_id_type=MESH)

    for j in range(1, Y):
        greet(z * Y + (y + j) % Y, d)
    loop(1, nz, lambda j: greet(((z + j) % nz) * Y + y, d))
    greet(e, core_to)
    for j in range(1, nx):
        greet(e, x_to(j))
    if nzh == 2:
        greet(e, zh_to)

    r0, r1 = routes_t[0:1, :], routes_t[1:2, :]
    eid = lax.broadcasted_iota(jnp.int32, (2 * nz, toks), 0)
    hit0, hit1 = (r0 == eid).astype(F32), (r1 == eid).astype(F32)
    upper = (
        lax.broadcasted_iota(jnp.int32, (toks, toks), 0) < lax.broadcasted_iota(jnp.int32, (toks, toks), 1)
    ).astype(BF)
    before = dot_nn((hit0 + hit1).astype(BF), upper)
    for k, (r, hit) in enumerate(((r0, hit0), (r1, hit1))):
        slot = jnp.sum(before * hit, axis=0, keepdims=True)
        meta[k : k + 1, :] = slot + ((r // 2) * msg).astype(F32)
        meta[2 + k : 3 + k, :] = (r % 2).astype(F32)
        meta[4 + k : 5 + k, :] = probs_t[k : k + 1, :]
    meta[6:8, :] = jnp.zeros((2, toks), F32)

    wd[0:feats, :] = w_down_t[...]
    wd[feats:, :] = jnp.zeros((w1 - feats, hidden), BF)

    pl.semaphore_wait(barrier, (Y - 1) + (nz - 1) + 1 + (nx - 1) + (1 if nzh == 2 else 0))

    sets = ((grad_t, r_grad), (meta, r_meta), (tok_t, r_tok))

    def y_copy(kind, j, i):
        src, dst = sets[kind]
        return remote(src, dst.at[i], sem_ys.at[kind * 2 + j], sem_yr.at[kind * 2 + i], z * Y + y // 2 + 2 * j, d)

    for j in range(2):
        to = y // 2 + 2 * j

        @pl.when(to != y)
        def _():
            for kind in range(3):
                y_copy(kind, j, h).start()

        @pl.when(to == y)
        def _():
            for src, dst in sets:
                dst[h] = src[...]

    for i in range(2):
        @pl.when(2 * h + i != y)
        def _():
            for kind in range(3):
                y_copy(kind, 0, i).wait_recv()

    targets = []
    parity = par.astype(F32)
    for k in range(2):
        for i in range(2):
            t = r_meta[i, k : k + 1, :] + float(cap * i)
            targets.append(jnp.where(r_meta[i, 2 + k : 3 + k, :] == parity, t, -1.0))
            lanes = pl.ds((2 * k + i) * toks, toks)
            scaled = r_grad[i].astype(F32) * r_meta[i, 4 + k : 5 + k, :]
            pack_b[0:feats, lanes] = scaled.astype(BF)
            pack_b[feats : 2 * feats, lanes] = r_tok[i]

    def z1_copy(c, j):
        to = send_z(c, j)
        return remote(sb1.at[to], x1.at[2 * z + h], sem_z1s.at[c * G + j], sem_z1r.at[c * G + j], to * Y + y, d)

    def z2_copy(c, j):
        to = send_z(c, j)
        return remote(sb2.at[to], x2.at[2 * z + h], sem_z2s.at[c * G + j], sem_z2r.at[c * G + j], to * Y + y, d)

    def f1_copy(c, j):
        at = 2 * recv_z(c, j) + h
        return remote(x1.at[at], x1.at[at], sem_f1s.at[c * G + j], sem_f1r.at[c * G + j], pair, d)

    def f2_copy(c, j):
        at = 2 * recv_z(c, j) + h
        return remote(x2.at[at], x2.at[at], sem_f2s.at[c * G + j], sem_f2r.at[c * G + j], pair, d)

    def first(c):
        return 1 if c == 0 else 0

    def pack(c):
        g = (zq + c) % C
        base = (g * (G * msg)).astype(F32)
        ids = lax.broadcasted_iota(jnp.int32, (G * msg, toks), 0).astype(F32) + base
        one_hot = jnp.concatenate([(t == ids).astype(BF) for t in targets], axis=1)
        packed = dot_nt(one_hot, pack_b[...]).astype(BF).reshape(G, msg, 2 * feats)
        sb1[pl.ds(g * G, G)] = packed[:, :, 0:w1]
        sb2[pl.ds(g * G, G)] = packed[:, :, w1:]
        if c == 0:
            x1[2 * z + h] = sb1[z]
            x2[2 * z + h] = sb2[z]
            f1_copy(0, 0).start()
        loop(first(c), G, lambda j: z1_copy(c, j).start())

    for c in range(C):
        pack(c)

    def activate(i):
        gv = s_gate[i].astype(F32)
        act[i] = (gv * jax.nn.sigmoid(gv) * s_up[i].astype(F32)).astype(BF)

    loop(0, 2 * nz, activate)

    def send_second(c):
        if c == 0:
            f2_copy(0, 0).start()
        loop(first(c), G, lambda j: z2_copy(c, j).start())

    def a_copy(c):
        return remote(pb.at[c, pl.ds((1 - core) * nx, nx)], ra.at[c], sem_as.at[c], sem_ar.at[c], e, core_to)

    def x_copy(c, j):
        k = c * (nx - 1) + j - 1
        return remote(qb.at[c, (x + j) % nx], rx.at[c, j - 1], sem_xs.at[k], sem_xr.at[k], e, x_to(j))

    def h_copy(c):
        return remote(wb.at[c], rz.at[c], sem_hs.at[c], sem_hr.at[c], e, zh_to)

    def g_copy(c, j):
        k = c * (nx - 1) + j - 1
        at = core * nx + x
        return remote(hid.at[c, at], hid.at[c, at], sem_gs.at[k], sem_gr.at[k], e, x_to(j))

    def c_copy(c):
        half = hid.at[c, pl.ds(core * nx, nx)]
        return remote(half, half, sem_cs.at[c], sem_cr.at[c], e, core_to)

    def p_copy(c):
        g = group(c)
        return remote(bg.at[1 - h, pl.ds(g * G, G)], rp.at[pl.ds(g * G, G)], sem_ps.at[c], sem_pr.at[c], pair, d)

    def r_copy(c, j):
        to = recv_z(c, j)
        return remote(ps.at[to], rr.at[z], sem_rs.at[c * G + j], sem_rr.at[c * G + j], to * Y + y, d)

    def stage_forward(c):
        def body(j):
            z1_copy(c, j).wait_recv()
            f1_copy(c, j).start()

        loop(first(c), G, body)

    def stage_product(c):
        loop(0, G, lambda j: f1_copy(c, j).wait_recv())
        g = group(c)
        left = x1[pl.ds(2 * G * g, 2 * G)].reshape(rows, w1)
        part = dot_nn(left, wd[...]).reshape(units, rows // units, hidden)
        p32[c] = part
        pb[c] = part.astype(BF)
        a_copy(c).start()

    def stage_core(c):
        a_copy(c).wait_recv()
        total = p32[c, pl.ds(core * nx, nx)] + ra[c].astype(F32)
        q32[c] = total
        qb[c] = total.astype(BF)
        for j in range(1, nx):
            x_copy(c, j).start()

    def stage_x(c):
        for j in range(1, nx):
            x_copy(c, j).wait_recv()
        total = q32[c, x]
        for j in range(1, nx):
            total = total + rx[c, j - 1].astype(F32)
        w32[c] = total
        wb[c] = total.astype(BF)
        if nzh == 2:
            h_copy(c).start()

    def stage_zh(c):
        total = w32[c]
        if nzh == 2:
            h_copy(c).wait_recv()
            total = total + rz[c].astype(F32)
        hid[c, core * nx + x] = total.astype(BF)
        for j in range(1, nx):
            g_copy(c, j).start()

    def stage_gather(c):
        for j in range(1, nx):
            g_copy(c, j).wait_recv()
        c_copy(c).start()

    def stage_hidden(c):
        c_copy(c).wait_recv()
        g = group(c)
        at = pl.ds(2 * G * g, 2 * G)
        back = hid[c].astype(F32).reshape(rows, hidden)
        gv = s_gate[at].astype(F32).reshape(rows, hidden)
        uv = s_up[at].astype(F32).reshape(rows, hidden)
        sig = jax.nn.sigmoid(gv)
        g_grad = (back * uv * sig * (1.0 + gv * (1.0 - sig))).astype(BF)
        u_grad = (back * gv * sig).astype(BF)
        gg[at] = g_grad.reshape(2 * G, msg, hidden)
        ug[at] = u_grad.reshape(2 * G, msg, hidden)
        block = (dot_nt(g_grad, w_gate[...]) + dot_nt(u_grad, w_up[...])).astype(BF)
        block = block.reshape(G, 2, msg, feats)
        bg[0, pl.ds(g * G, G)] = block[:, 0]
        bg[1, pl.ds(g * G, G)] = block[:, 1]
        p_copy(c).start()

    def stage_pair(c):
        p_copy(c).wait_recv()
        at = pl.ds(group(c) * G, G)
        ps[at] = (bg[h, at].astype(F32) + rp[at].astype(F32)).astype(BF)
        if c == 0:
            rr[z] = ps[z]
        loop(first(c), G, lambda j: r_copy(c, j).start())

    def stage_second(c):
        send_second(c)

    stages = [
        stage_forward, stage_product, stage_core, stage_x, stage_second, stage_zh,
        stage_gather, stage_hidden, stage_pair,
    ]
    for step in range(C + len(stages) - 1):
        for s in reversed(range(len(stages))):
            c = step - s
            if 0 <= c < C:
                stages[s](c)

    for c in range(C):
        def forward2(j):
            z2_copy(c, j).wait_recv()
            f2_copy(c, j).start()

        loop(first(c), G, forward2)

    total_rows = 2 * nz * msg
    right = act[...].reshape(total_rows, hidden)
    for m in range(w1 // 128):
        lo, hi = m * 128, min((m + 1) * 128, feats)
        left = x1[:, :, m * 128 : (m + 1) * 128].reshape(total_rows, 128)
        o_down[lo:hi, :] = dot_tn(left, right)[0 : hi - lo].astype(BF)

    for c in range(C):
        loop(0, G, lambda j: f2_copy(c, j).wait_recv())
    skip = 128 - (w1 - feats)
    for grads, out in ((gg, o_gate), (ug, o_up)):
        right = grads[...].reshape(total_rows, hidden)
        left = x1[:, :, w1 - 128 : w1].reshape(total_rows, 128)
        out[0 : 128 - skip, :] = dot_tn(left, right)[skip:].astype(BF)
        for m in range((2 * feats - w1) // 128):
            left = x2[:, :, m * 128 : (m + 1) * 128].reshape(total_rows, 128)
            lo = 128 - skip + m * 128
            out[lo : lo + 128, :] = dot_tn(left, right).astype(BF)

    for c in range(C):
        loop(first(c), G, lambda j: r_copy(c, j).wait_recv())
    ids = lax.broadcasted_iota(jnp.int32, (nz * msg, toks), 0).astype(F32)
    back_rows = rr[...].reshape(nz * msg, feats)

    def o_copy(i, j):
        return remote(ot.at[i], ro.at[par], sem_os.at[i], sem_or.at[j], z * Y + 2 * h + i, d)

    for i in range(2):
        pick = ((targets[i] == ids).astype(F32) + (targets[2 + i] == ids).astype(F32)).astype(BF)
        ot[i] = dot_tn(back_rows, pick).astype(BF)
        s = 2 * h + i

        for p in range(2):
            @pl.when((s != y) & (par == p))
            def _():
                o_copy(i, p).start()

        @pl.when(s == y)
        def _():
            ro[par] = ot[i]

    for j in range(2):
        @pl.when(y // 2 + 2 * j != y)
        def _():
            o_copy(0, j).wait_recv()

    o_tok[...] = (ro[0].astype(F32) + ro[1].astype(F32)).astype(BF)

    for j in range(2):
        @pl.when(y // 2 + 2 * j != y)
        def _():
            for kind in range(3):
                y_copy(kind, j, h).wait_send()

    for c in range(C):
        def sent(j):
            z1_copy(c, j).wait_send()
            z2_copy(c, j).wait_send()
            r_copy(c, j).wait_send()

        loop(first(c), G, sent)

        def forwarded(j):
            f1_copy(c, j).wait_send()
            f2_copy(c, j).wait_send()

        loop(0, G, forwarded)
        a_copy(c).wait_send()
        for j in range(1, nx):
            x_copy(c, j).wait_send()
            g_copy(c, j).wait_send()
        if nzh == 2:
            h_copy(c).wait_send()
        c_copy(c).wait_send()
        p_copy(c).wait_send()
    for i in range(2):
        @pl.when(2 * h + i != y)
        def _():
            o_copy(i, 0).wait_send()


def shards(dp_shape, chunks, tokens_in, grad_out, routes, gate_probs, saved_gate, saved_up, w_gate, w_up, w_down):
    groups = lax.axis_size("expert")
    nx, nzh = dp_shape
    nz = groups // Y
    slot_rows, hidden = saved_gate.shape[1:]
    cap = slot_rows // groups
    toks, feats = tokens_in.shape
    msg = 2 * cap
    C = chunks
    G = nz // C
    w1 = -(-feats // 128) * 128
    w2 = 2 * feats - w1
    units = 2 * nx
    unit = 2 * G * msg // units
    dma = lambda n: pltpu.SemaphoreType.DMA((n,))
    vm = lambda shape, dtype=BF: pltpu.VMEM(shape, dtype)
    scratch = [
        vm((8, toks), F32), vm((2, feats, toks)), vm((2, feats, toks)), vm((2, 8, toks), F32),
        vm((2 * feats, 4 * toks)),
        vm((nz, msg, w1)), vm((nz, msg, w2)), vm((2 * nz, msg, w1)), vm((2 * nz, msg, w2)),
        vm((w1, hidden)), vm((2 * nz, msg, hidden)),
        vm((C, units, unit, hidden), F32), vm((C, units, unit, hidden)), vm((C, nx, unit, hidden)),
        vm((C, nx, unit, hidden), F32), vm((C, nx, unit, hidden)), vm((C, max(nx - 1, 1), unit, hidden)),
        vm((C, unit, hidden), F32), vm((C, unit, hidden)), vm((C, unit, hidden)),
        vm((C, units, unit, hidden)),
        vm((2 * nz, msg, hidden)), vm((2 * nz, msg, hidden)),
        vm((2, nz, msg, feats)), vm((nz, msg, feats)), vm((nz, msg, feats)), vm((nz, msg, feats)),
        vm((2, feats, toks)), vm((2, feats, toks)),
        dma(6), dma(6), dma(nz), dma(nz), dma(nz), dma(nz), dma(nz), dma(nz), dma(nz), dma(nz),
        dma(C), dma(C), dma(C * max(nx - 1, 1)), dma(C * max(nx - 1, 1)), dma(C), dma(C),
        dma(C * max(nx - 1, 1)), dma(C * max(nx - 1, 1)), dma(C), dma(C),
        dma(C), dma(C), dma(nz), dma(nz), dma(2), dma(2),
    ]
    o_tok, o_gate, o_up, o_down = pl.pallas_call(
        functools.partial(kernel, (nz, nx, nzh, cap, C)),
        out_shape=(
            jax.ShapeDtypeStruct((feats, toks), BF),
            jax.ShapeDtypeStruct((feats, hidden), BF),
            jax.ShapeDtypeStruct((feats, hidden), BF),
            jax.ShapeDtypeStruct((feats, hidden), BF),
        ),
        in_specs=[pl.BlockSpec(memory_space=pltpu.VMEM)] * 9,
        out_specs=(pl.BlockSpec(memory_space=pltpu.VMEM),) * 4,
        scratch_shapes=scratch,
        compiler_params=pltpu.CompilerParams(
            collective_id=0, has_side_effects=True, vmem_limit_bytes=48 * 1024 * 1024
        ),
    )(
        tokens_in.T, grad_out.T, routes.T, gate_probs.T,
        saved_gate.reshape(2 * nz, msg, hidden), saved_up.reshape(2 * nz, msg, hidden),
        w_gate[0], w_up[0], w_down[0].T,
    )
    return o_tok.T, o_gate[None], o_up[None], o_down.T[None]


def build(mesh, dp_shape, chunks):
    return jax.shard_map(
        functools.partial(shards, dp_shape, chunks),
        mesh=mesh,
        in_specs=(
            P("expert", "dp"),
            P("expert", "dp"),
            P("expert", None),
            P("expert", None),
            P("expert", None, None),
            P("expert", None, None),
            P("expert", "dp", None),
            P("expert", "dp", None),
            P("expert", None, "dp"),
        ),
        out_specs=(
            P("expert", "dp"),
            P("expert", "dp", None),
            P("expert", "dp", None),
            P("expert", None, "dp"),
        ),
        check_vma=False,
    )


def solution(mesh):
    return build(mesh, (4, 2), CHUNKS)
```

```python
import functools

import jax
import jax.numpy as jnp
from jax import lax
from jax.experimental import pallas as pl
from jax.experimental.pallas import tpu as pltpu
from jax.sharding import PartitionSpec as P

MESH = pl.DeviceIdType.MESH
Y = 4
CHUNKS = 2
BF = jnp.bfloat16
F32 = jnp.float32


def dot_nn(a, b):
    return lax.dot_general(a, b, (((1,), (0,)), ((), ())), preferred_element_type=F32)


def dot_nt(a, b):
    return lax.dot_general(a, b, (((1,), (1,)), ((), ())), preferred_element_type=F32)


def dot_tn(a, b):
    return lax.dot_general(a, b, (((0,), (0,)), ((), ())), preferred_element_type=F32)


def kernel(
    cfg,
    tok_t, grad_t, routes_t, probs_t, h_gate, h_up, h_wg, h_wu, h_wd,
    o_tok, o_gate, o_up, o_down,
    s_gate, s_up, w_gate, w_up, sem_in,
    meta, r_tok, r_grad, r_meta, pack_b, pack_c,
    sb1, sb2, x1, x2, wd, act,
    p32, pb, rx, w32, wb, rz, hid,
    xt, wt, out32, gg, ug, bg, rp, ps, rr, ot, ro,
    sem_ys, sem_yr, sem_z1s, sem_z1r, sem_f1s, sem_f1r, sem_z2s, sem_z2r, sem_f2s, sem_f2r,
    sem_xs, sem_xr, sem_hs, sem_hr, sem_gs, sem_gr,
    sem_ps, sem_pr, sem_rs, sem_rr, sem_os, sem_or,
):
    nz, nx, nzh, cap, C = cfg
    G = nz // C
    feats, toks = tok_t.shape
    hidden = h_gate.shape[2]
    w1 = sb1.shape[2]
    msg = 2 * cap
    units = 2 * nx
    rows = 2 * G * msg

    e = lax.axis_index("expert")
    d = lax.axis_index("dp")
    y, z = lax.rem(e, Y), lax.div(e, Y)
    core, zh, x = lax.rem(d, 2), lax.rem(lax.div(d, 2), nzh), lax.div(d, 2 * nzh)
    par, h = lax.div(y, 2), lax.rem(y, 2)
    zq, zr = lax.div(z, G), lax.rem(z, G)
    pair = z * Y + (y + 1 - 2 * h)
    me = core * nx + x
    zh_to = (x * nzh + (1 - zh)) * 2 + core

    def dp_to(j):
        v = lax.rem(me + j, units)
        return (lax.rem(v, nx) * nzh + zh) * 2 + lax.div(v, nx)

    def send_z(c, j):
        return lax.rem(zq + c, C) * G + lax.rem(zr + j, G)

    def recv_z(c, j):
        return lax.rem(zq + (C - c), C) * G + lax.rem(zr + G - j, G)

    def group(c):
        return lax.rem(zq + (C - c), C)

    def remote(src, dst, ss, rs, ee, dd):
        return pltpu.make_async_remote_copy(
            src_ref=src, dst_ref=dst, send_sem=ss, recv_sem=rs,
            device_id=(ee, dd), device_id_type=MESH,
        )

    def loop(lo, hi, body):
        if hi - lo == 1:
            body(lo)
        elif hi > lo:
            lax.fori_loop(lo, hi, lambda i, _: (body(i), 0)[1], 0)

    ins = [
        pltpu.make_async_copy(src, dst, sem_in.at[n])
        for n, (src, dst) in enumerate(
            ((h_gate, s_gate), (h_up, s_up), (h_wd, wd.at[0:feats]), (h_wg, w_gate), (h_wu, w_up))
        )
    ]
    for copy in ins:
        copy.start()
    wd[feats:, :] = jnp.zeros((w1 - feats, hidden), BF)

    barrier = pltpu.get_barrier_semaphore()

    def greet(ee, dd):
        pl.semaphore_signal(barrier, inc=1, device_id=(ee, dd), device_id_type=MESH)

    for j in range(1, Y):
        greet(z * Y + (y + j) % Y, d)
    loop(1, nz, lambda j: greet(lax.rem(z + j, nz) * Y + y, d))
    loop(1, units, lambda j: greet(e, dp_to(j)))
    if nzh == 2:
        greet(e, zh_to)

    r0, r1 = routes_t[0:1, :], routes_t[1:2, :]
    eid = lax.broadcasted_iota(jnp.int32, (2 * nz, toks), 0)
    hit0, hit1 = (r0 == eid).astype(F32), (r1 == eid).astype(F32)
    upper = (
        lax.broadcasted_iota(jnp.int32, (toks, toks), 0) < lax.broadcasted_iota(jnp.int32, (toks, toks), 1)
    ).astype(BF)
    before = dot_nn((hit0 + hit1).astype(BF), upper)
    for k, (r, hit) in enumerate(((r0, hit0), (r1, hit1))):
        slot = jnp.sum(before * hit, axis=0, keepdims=True)
        meta[k : k + 1, :] = slot + ((r // 2) * msg).astype(F32)
        meta[2 + k : 3 + k, :] = (r % 2).astype(F32)
        meta[4 + k : 5 + k, :] = probs_t[k : k + 1, :]
    meta[6:8, :] = jnp.zeros((2, toks), F32)

    pl.semaphore_wait(barrier, (Y - 1) + (nz - 1) + (units - 1) + (1 if nzh == 2 else 0))

    lead = w1 - feats
    sets = (
        (grad_t, lambda i: r_grad.at[i]),
        (meta, lambda i: r_meta.at[i]),
        (tok_t.at[0:lead], lambda i: r_tok.at[i, 0:lead]),
        (tok_t.at[lead:feats], lambda i: r_tok.at[i, lead:feats]),
    )

    def y_copy(kind, j, i):
        src, dst = sets[kind]
        return remote(src, dst(i), sem_ys.at[kind * 2 + j], sem_yr.at[kind * 2 + i], z * Y + y // 2 + 2 * j, d)

    for j in range(2):
        to = y // 2 + 2 * j

        @pl.when(to != y)
        def _():
            for kind in range(4):
                y_copy(kind, j, h).start()

        @pl.when(to == y)
        def _():
            r_grad[h] = grad_t[...]
            r_meta[h] = meta[...]
            r_tok[h] = tok_t[...]

    for i in range(2):
        @pl.when(2 * h + i != y)
        def _():
            for kind in range(3):
                y_copy(kind, 0, i).wait_recv()

    targets = []
    parity = par.astype(F32)
    for k in range(2):
        for i in range(2):
            t = r_meta[i, k : k + 1, :] + float(cap * i)
            targets.append(jnp.where(r_meta[i, 2 + k : 3 + k, :] == parity, t, -1.0))
            lanes = pl.ds((2 * k + i) * toks, toks)
            scaled = r_grad[i].astype(F32) * r_meta[i, 4 + k : 5 + k, :]
            both = jnp.concatenate([scaled.astype(BF), r_tok[i, 0:lead]], axis=0)
            pack_b[lanes, :] = both.T

    def z1_copy(c, j):
        to = send_z(c, j)
        return remote(sb1.at[to], x1.at[2 * z + h], sem_z1s.at[c * G + j], sem_z1r.at[c * G + j], to * Y + y, d)

    def z2_copy(c, j):
        to = send_z(c, j)
        return remote(sb2.at[to], x2.at[2 * z + h], sem_z2s.at[c * G + j], sem_z2r.at[c * G + j], to * Y + y, d)

    def f1_copy(c, j):
        at = 2 * recv_z(c, j) + h
        return remote(x1.at[at], x1.at[at], sem_f1s.at[c * G + j], sem_f1r.at[c * G + j], pair, d)

    def f2_copy(c, j):
        at = 2 * recv_z(c, j) + h
        return remote(x2.at[at], x2.at[at], sem_f2s.at[c * G + j], sem_f2r.at[c * G + j], pair, d)

    def first(c):
        return 1 if c == 0 else 0

    def pack(c):
        g = lax.rem(zq + c, C)
        base = (g * (G * msg)).astype(F32)
        ids = lax.broadcasted_iota(jnp.int32, (G * msg, toks), 0).astype(F32) + base
        one_hot = jnp.concatenate([(t == ids).astype(BF) for t in targets], axis=1)
        sb1[pl.ds(g * G, G)] = dot_nn(one_hot, pack_b[...]).astype(BF).reshape(G, msg, w1)
        if c == 0:
            x1[2 * z + h] = sb1[z]
            f1_copy(0, 0).start()
        loop(first(c), G, lambda j: z1_copy(c, j).start())

    for c in range(C):
        pack(c)

    for copy in ins:
        copy.wait()

    total_rows = 2 * nz * msg

    def fill_weights():
        for n, ref in enumerate((w_gate, w_up)):
            wt[n * hidden : (n + 1) * hidden, :] = ref[...].T

    def fill_activation():
        def body(i):
            gv = s_gate[i].astype(F32)
            act[i] = (gv * jax.nn.sigmoid(gv) * s_up[i].astype(F32)).astype(BF)

        loop(0, 2 * nz, body)

    def turn(ref, lo):
        for m in range(ref.shape[2] // 128):
            at = lo + m * 128
            xt[at : at + 128, :] = ref[:, :, m * 128 : (m + 1) * 128].reshape(total_rows, 128).T

    def fill_down():
        turn(x1, 0)
        o_down[...] = dot_nn(xt[0:feats, :], act[...].reshape(total_rows, hidden)).astype(BF)

    def fill_second():
        for i in range(2):
            @pl.when(2 * h + i != y)
            def _():
                y_copy(3, 0, i).wait_recv()

        for i in range(2):
            pack_c[i * toks : (i + 1) * toks, :] = r_tok[i, lead:feats].T

    def picks(c):
        g = lax.rem(zq + c, C)
        ids = lax.broadcasted_iota(jnp.int32, (G * msg, toks), 0).astype(F32) + (g * (G * msg)).astype(F32)
        both = [((targets[i] == ids).astype(F32) + (targets[2 + i] == ids).astype(F32)).astype(BF) for i in range(2)]
        return g, jnp.concatenate(both, axis=1)

    def send_second(c):
        g, one_hot = picks(c)
        sb2[pl.ds(g * G, G)] = dot_nn(one_hot, pack_c[...]).astype(BF).reshape(G, msg, 2 * feats - w1)
        if c == 0:
            x2[2 * z + h] = sb2[z]
            f2_copy(0, 0).start()
        loop(first(c), G, lambda j: z2_copy(c, j).start())

    def x_copy(c, j):
        k = c * (units - 1) + j - 1
        return remote(pb.at[c, lax.rem(me + j, units)], rx.at[c, j - 1], sem_xs.at[k], sem_xr.at[k], e, dp_to(j))

    def h_copy(c):
        return remote(wb.at[c], rz.at[c], sem_hs.at[c], sem_hr.at[c], e, zh_to)

    def g_copy(c, j):
        k = c * (units - 1) + j - 1
        return remote(hid.at[c, me], hid.at[c, me], sem_gs.at[k], sem_gr.at[k], e, dp_to(j))

    def p_copy(c):
        g = group(c)
        return remote(bg.at[1 - h, pl.ds(g * G, G)], rp.at[pl.ds(g * G, G)], sem_ps.at[c], sem_pr.at[c], pair, d)

    def r_copy(c, j):
        to = recv_z(c, j)
        return remote(ps.at[to], rr.at[z], sem_rs.at[c * G + j], sem_rr.at[c * G + j], to * Y + y, d)

    def stage_forward(c):
        def body(j):
            z1_copy(c, j).wait_recv()
            f1_copy(c, j).start()

        loop(first(c), G, body)

    def stage_product(c):
        loop(0, G, lambda j: f1_copy(c, j).wait_recv())
        g = group(c)
        left = x1[pl.ds(2 * G * g, 2 * G)].reshape(rows, w1)
        part = dot_nn(left, wd[...]).reshape(units, rows // units, hidden)
        p32[c] = part
        pb[c] = part.astype(BF)
        loop(1, units, lambda j: x_copy(c, j).start())

    def stage_sum(c):
        loop(1, units, lambda j: x_copy(c, j).wait_recv())
        total = p32[c, me]
        for j in range(1, units):
            total = total + rx[c, j - 1].astype(F32)
        w32[c] = total
        if nzh == 2:
            wb[c] = total.astype(BF)
            h_copy(c).start()

    def stage_zh(c):
        total = w32[c]
        if nzh == 2:
            h_copy(c).wait_recv()
            total = total + rz[c].astype(F32)
        hid[c, me] = total.astype(BF)
        loop(1, units, lambda j: g_copy(c, j).start())

    def stage_hidden(c):
        loop(1, units, lambda j: g_copy(c, j).wait_recv())
        g = group(c)
        at = pl.ds(2 * G * g, 2 * G)
        back = hid[c].astype(F32).reshape(rows, hidden)
        gv = s_gate[at].astype(F32).reshape(rows, hidden)
        uv = s_up[at].astype(F32).reshape(rows, hidden)
        sig = jax.nn.sigmoid(gv)
        g_grad = (back * uv * sig * (1.0 + gv * (1.0 - sig))).astype(BF)
        u_grad = (back * gv * sig).astype(BF)
        joined = jnp.concatenate([g_grad, u_grad], axis=1)
        gg[at] = g_grad.reshape(2 * G, msg, hidden)
        ug[at] = u_grad.reshape(2 * G, msg, hidden)
        block = dot_nn(joined, wt[...]).astype(BF).reshape(G, 2, msg, feats)
        bg[0, pl.ds(g * G, G)] = block[:, 0]
        bg[1, pl.ds(g * G, G)] = block[:, 1]
        p_copy(c).start()

    def stage_pair(c):
        p_copy(c).wait_recv()
        at = pl.ds(group(c) * G, G)
        ps[at] = (bg[h, at].astype(F32) + rp[at].astype(F32)).astype(BF)
        if c == 0:
            rr[z] = ps[z]
        loop(first(c), G, lambda j: r_copy(c, j).start())

    def stage_second(c):
        send_second(c)

    stages = [stage_forward, stage_product, stage_sum, stage_second, stage_zh, stage_hidden, stage_pair]
    fillers = {0: fill_second, 1: fill_weights, 2: fill_activation, C + 1: fill_down}
    for step in range(C + len(stages) - 1):
        for s in reversed(range(len(stages))):
            c = step - s
            if 0 <= c < C:
                stages[s](c)
        if step in fillers:
            fillers[step]()

    for c in range(C):
        def forward2(j):
            z2_copy(c, j).wait_recv()
            f2_copy(c, j).start()

        loop(first(c), G, forward2)

    for c in range(C):
        loop(0, G, lambda j: f2_copy(c, j).wait_recv())
    turn(x2, w1)
    for grads, out in ((gg, o_gate), (ug, o_up)):
        out[...] = dot_nn(xt[feats : 2 * feats, :], grads[...].reshape(total_rows, hidden)).astype(BF)

    for c in range(C):
        loop(first(c), G, lambda j: r_copy(c, j).wait_recv())
        g, one_hot = picks(c)
        back_rows = rr[pl.ds(g * G, G)].reshape(G * msg, feats)
        part = dot_tn(back_rows, one_hot)
        out32[...] = part if c == 0 else out32[...] + part

    def o_copy(i, j):
        return remote(ot.at[i], ro.at[par], sem_os.at[i], sem_or.at[j], z * Y + 2 * h + i, d)

    for i in range(2):
        ot[i] = out32[:, i * toks : (i + 1) * toks].astype(BF)
        s = 2 * h + i

        for p in range(2):
            @pl.when((s != y) & (par == p))
            def _():
                o_copy(i, p).start()

        @pl.when(s == y)
        def _():
            ro[par] = ot[i]

    for j in range(2):
        @pl.when(y // 2 + 2 * j != y)
        def _():
            o_copy(0, j).wait_recv()

    o_tok[...] = (ro[0].astype(F32) + ro[1].astype(F32)).astype(BF)

    for j in range(2):
        @pl.when(y // 2 + 2 * j != y)
        def _():
            for kind in range(4):
                y_copy(kind, j, h).wait_send()

    for c in range(C):
        def sent(j):
            z1_copy(c, j).wait_send()
            z2_copy(c, j).wait_send()
            r_copy(c, j).wait_send()

        loop(first(c), G, sent)

        def forwarded(j):
            f1_copy(c, j).wait_send()
            f2_copy(c, j).wait_send()

        loop(0, G, forwarded)
        loop(1, units, lambda j: (x_copy(c, j).wait_send(), g_copy(c, j).wait_send()))
        if nzh == 2:
            h_copy(c).wait_send()
        p_copy(c).wait_send()
    for i in range(2):
        @pl.when(2 * h + i != y)
        def _():
            o_copy(i, 0).wait_send()


def shards(dp_shape, chunks, tokens_in, grad_out, routes, gate_probs, saved_gate, saved_up, w_gate, w_up, w_down):
    groups = lax.axis_size("expert")
    nx, nzh = dp_shape
    nz = groups // Y
    slot_rows, hidden = saved_gate.shape[1:]
    cap = slot_rows // groups
    toks, feats = tokens_in.shape
    msg = 2 * cap
    C = chunks
    G = nz // C
    w1 = -(-feats // 128) * 128
    w2 = 2 * feats - w1
    units = 2 * nx
    unit = 2 * G * msg // units
    dma = lambda n: pltpu.SemaphoreType.DMA((n,))
    vm = lambda shape, dtype=BF: pltpu.VMEM(shape, dtype)
    scratch = [
        vm((2 * nz, msg, hidden)), vm((2 * nz, msg, hidden)), vm((feats, hidden)), vm((feats, hidden)), dma(5),
        vm((8, toks), F32), vm((2, feats, toks)), vm((2, feats, toks)), vm((2, 8, toks), F32),
        vm((4 * toks, w1)), vm((2 * toks, w2)),
        vm((nz, msg, w1)), vm((nz, msg, w2)), vm((2 * nz, msg, w1)), vm((2 * nz, msg, w2)),
        vm((w1, hidden)), vm((2 * nz, msg, hidden)),
        vm((C, units, unit, hidden), F32), vm((C, units, unit, hidden)), vm((C, units - 1, unit, hidden)),
        vm((C, unit, hidden), F32), vm((C, unit, hidden)), vm((C, unit, hidden)),
        vm((C, units, unit, hidden)),
        vm((2 * feats, 2 * nz * msg)), vm((2 * hidden, feats)), vm((feats, 2 * toks), F32),
        vm((2 * nz, msg, hidden)), vm((2 * nz, msg, hidden)),
        vm((2, nz, msg, feats)), vm((nz, msg, feats)), vm((nz, msg, feats)), vm((nz, msg, feats)),
        vm((2, feats, toks)), vm((2, feats, toks)),
        dma(8), dma(8), dma(nz), dma(nz), dma(nz), dma(nz), dma(nz), dma(nz), dma(nz), dma(nz),
        dma(C * (units - 1)), dma(C * (units - 1)), dma(C), dma(C), dma(C * (units - 1)), dma(C * (units - 1)),
        dma(C), dma(C), dma(nz), dma(nz), dma(2), dma(2),
    ]
    o_tok, o_gate, o_up, o_down = pl.pallas_call(
        functools.partial(kernel, (nz, nx, nzh, cap, C)),
        out_shape=(
            jax.ShapeDtypeStruct((feats, toks), BF),
            jax.ShapeDtypeStruct((feats, hidden), BF),
            jax.ShapeDtypeStruct((feats, hidden), BF),
            jax.ShapeDtypeStruct((feats, hidden), BF),
        ),
        in_specs=[pl.BlockSpec(memory_space=pltpu.VMEM)] * 4 + [pl.BlockSpec(memory_space=pltpu.HBM)] * 5,
        out_specs=(pl.BlockSpec(memory_space=pltpu.VMEM),) * 4,
        scratch_shapes=scratch,
        compiler_params=pltpu.CompilerParams(
            collective_id=0, has_side_effects=True, vmem_limit_bytes=60 * 1024 * 1024
        ),
    )(
        tokens_in.T, grad_out.T, routes.T, gate_probs.T,
        saved_gate.reshape(2 * nz, msg, hidden), saved_up.reshape(2 * nz, msg, hidden),
        w_gate[0], w_up[0], w_down[0].T,
    )
    return o_tok.T, o_gate[None], o_up[None], o_down.T[None]


def build(mesh, dp_shape, chunks):
    return jax.shard_map(
        functools.partial(shards, dp_shape, chunks),
        mesh=mesh,
        in_specs=(
            P("expert", "dp"),
            P("expert", "dp"),
            P("expert", None),
            P("expert", None),
            P("expert", None, None),
            P("expert", None, None),
            P("expert", "dp", None),
            P("expert", "dp", None),
            P("expert", None, "dp"),
        ),
        out_specs=(
            P("expert", "dp"),
            P("expert", "dp", None),
            P("expert", "dp", None),
            P("expert", None, "dp"),
        ),
        check_vma=False,
    )


def solution(mesh):
    return build(mesh, (4, 2), CHUNKS)
```

```python
import functools

import jax
import jax.numpy as jnp
from jax import lax
from jax.experimental import pallas as pl
from jax.experimental.pallas import tpu as pltpu
from jax.sharding import PartitionSpec as P

MESH = pl.DeviceIdType.MESH
Y = 4
CHUNKS = 2
BF = jnp.bfloat16
F32 = jnp.float32


def dot_nn(a, b):
    return lax.dot_general(a, b, (((1,), (0,)), ((), ())), preferred_element_type=F32)


def dot_nt(a, b):
    return lax.dot_general(a, b, (((1,), (1,)), ((), ())), preferred_element_type=F32)


def dot_tn(a, b):
    return lax.dot_general(a, b, (((0,), (0,)), ((), ())), preferred_element_type=F32)


def kernel(
    cfg,
    tok_t, grad_t, routes_t, probs_t, h_gate, h_up, h_wg, h_wu, h_wd,
    o_tok, o_gate, o_up, o_down,
    s_gate, s_up, w_gate, w_up, sem_in,
    meta, r_tok, r_grad, r_meta, pack_b, pack_c,
    sb1, sb2, x1, x2, wd, act,
    p32, pb, rx, w32, wb, rz, hid,
    xt, wt, out32, gg, ug, bg, rp, ps, pt, rr, rt, ot, ro,
    sem_ys, sem_yr, sem_z1s, sem_z1r, sem_f1s, sem_f1r, sem_z2s, sem_z2r, sem_f2s, sem_f2r,
    sem_xs, sem_xr, sem_hs, sem_hr, sem_gs, sem_gr,
    sem_ps, sem_pr, sem_rs, sem_rr, sem_ts, sem_tr, sem_os, sem_or,
):
    nz, nx, nzh, cap, C = cfg
    G = nz // C
    feats, toks = tok_t.shape
    hidden = h_gate.shape[2]
    w1 = sb1.shape[2]
    msg = 2 * cap
    units = 2 * nx
    rows = 2 * G * msg
    wide, half = ps.shape[2], pt.shape[1]

    e = lax.axis_index("expert")
    d = lax.axis_index("dp")
    y, z = lax.rem(e, Y), lax.div(e, Y)
    core, zh, x = lax.rem(d, 2), lax.rem(lax.div(d, 2), nzh), lax.div(d, 2 * nzh)
    par, h = lax.div(y, 2), lax.rem(y, 2)
    zq, zr = lax.div(z, G), lax.rem(z, G)
    pair = z * Y + (y + 1 - 2 * h)
    me = core * nx + x
    zh_to = (x * nzh + (1 - zh)) * 2 + core

    def dp_to(j):
        v = lax.rem(me + j, units)
        return (lax.rem(v, nx) * nzh + zh) * 2 + lax.div(v, nx)

    def send_z(c, j):
        return lax.rem(zq + c, C) * G + lax.rem(zr + j, G)

    def recv_z(c, j):
        return lax.rem(zq + (C - c), C) * G + lax.rem(zr + G - j, G)

    def group(c):
        return lax.rem(zq + (C - c), C)

    def remote(src, dst, ss, rs, ee, dd):
        return pltpu.make_async_remote_copy(
            src_ref=src, dst_ref=dst, send_sem=ss, recv_sem=rs,
            device_id=(ee, dd), device_id_type=MESH,
        )

    def loop(lo, hi, body):
        if hi - lo == 1:
            body(lo)
        elif hi > lo:
            lax.fori_loop(lo, hi, lambda i, _: (body(i), 0)[1], 0)

    ins = [
        pltpu.make_async_copy(src, dst, sem_in.at[n])
        for n, (src, dst) in enumerate(
            ((h_gate, s_gate), (h_up, s_up), (h_wd, wd.at[0:feats]), (h_wg, w_gate), (h_wu, w_up))
        )
    ]
    for copy in ins:
        copy.start()
    wd[feats:, :] = jnp.zeros((w1 - feats, hidden), BF)

    barrier = pltpu.get_barrier_semaphore()

    def greet(ee, dd):
        pl.semaphore_signal(barrier, inc=1, device_id=(ee, dd), device_id_type=MESH)

    for j in range(1, Y):
        greet(z * Y + (y + j) % Y, d)
    loop(1, nz, lambda j: greet(lax.rem(z + j, nz) * Y + y, d))
    loop(1, units, lambda j: greet(e, dp_to(j)))
    if nzh == 2:
        greet(e, zh_to)

    r0, r1 = routes_t[0:1, :], routes_t[1:2, :]
    eid = lax.broadcasted_iota(jnp.int32, (2 * nz, toks), 0)
    hit0, hit1 = (r0 == eid).astype(F32), (r1 == eid).astype(F32)
    upper = (
        lax.broadcasted_iota(jnp.int32, (toks, toks), 0) < lax.broadcasted_iota(jnp.int32, (toks, toks), 1)
    ).astype(BF)
    before = dot_nn((hit0 + hit1).astype(BF), upper)
    for k, (r, hit) in enumerate(((r0, hit0), (r1, hit1))):
        slot = jnp.sum(before * hit, axis=0, keepdims=True)
        meta[k : k + 1, :] = slot + ((r // 2) * msg).astype(F32)
        meta[2 + k : 3 + k, :] = (r % 2).astype(F32)
        meta[4 + k : 5 + k, :] = probs_t[k : k + 1, :]
    meta[6:8, :] = jnp.zeros((2, toks), F32)

    pl.semaphore_wait(barrier, (Y - 1) + (nz - 1) + (units - 1) + (1 if nzh == 2 else 0))

    lead = w1 - feats
    sets = (
        (grad_t, lambda i: r_grad.at[i]),
        (meta, lambda i: r_meta.at[i]),
        (tok_t.at[0:lead], lambda i: r_tok.at[i, 0:lead]),
        (tok_t.at[lead:feats], lambda i: r_tok.at[i, lead:feats]),
    )

    def y_copy(kind, j, i):
        src, dst = sets[kind]
        return remote(src, dst(i), sem_ys.at[kind * 2 + j], sem_yr.at[kind * 2 + i], z * Y + y // 2 + 2 * j, d)

    for j in range(2):
        to = y // 2 + 2 * j

        @pl.when(to != y)
        def _():
            for kind in range(4):
                y_copy(kind, j, h).start()

        @pl.when(to == y)
        def _():
            r_grad[h] = grad_t[...]
            r_meta[h] = meta[...]
            r_tok[h] = tok_t[...]

    for i in range(2):
        @pl.when(2 * h + i != y)
        def _():
            for kind in range(3):
                y_copy(kind, 0, i).wait_recv()

    targets = []
    parity = par.astype(F32)
    for k in range(2):
        for i in range(2):
            t = r_meta[i, k : k + 1, :] + float(cap * i)
            targets.append(jnp.where(r_meta[i, 2 + k : 3 + k, :] == parity, t, -1.0))
            lanes = pl.ds((2 * k + i) * toks, toks)
            scaled = r_grad[i].astype(F32) * r_meta[i, 4 + k : 5 + k, :]
            both = jnp.concatenate([scaled.astype(BF), r_tok[i, 0:lead]], axis=0)
            pack_b[lanes, :] = both.T

    def z1_copy(c, j):
        to = send_z(c, j)
        return remote(sb1.at[to], x1.at[2 * z + h], sem_z1s.at[c * G + j], sem_z1r.at[c * G + j], to * Y + y, d)

    def z2_copy(c, j):
        to = send_z(c, j)
        return remote(sb2.at[to], x2.at[2 * z + h], sem_z2s.at[c * G + j], sem_z2r.at[c * G + j], to * Y + y, d)

    def f1_copy(c, j):
        at = 2 * recv_z(c, j) + h
        return remote(x1.at[at], x1.at[at], sem_f1s.at[c * G + j], sem_f1r.at[c * G + j], pair, d)

    def f2_copy(c, j):
        at = 2 * recv_z(c, j) + h
        return remote(x2.at[at], x2.at[at], sem_f2s.at[c * G + j], sem_f2r.at[c * G + j], pair, d)

    def first(c):
        return 1 if c == 0 else 0

    def pack(c):
        g = lax.rem(zq + c, C)
        base = (g * (G * msg)).astype(F32)
        ids = lax.broadcasted_iota(jnp.int32, (G * msg, toks), 0).astype(F32) + base
        one_hot = jnp.concatenate([(t == ids).astype(BF) for t in targets], axis=1)
        sb1[pl.ds(g * G, G)] = dot_nn(one_hot, pack_b[...]).astype(BF).reshape(G, msg, w1)
        if c == 0:
            x1[2 * z + h] = sb1[z]
            f1_copy(0, 0).start()
        loop(first(c), G, lambda j: z1_copy(c, j).start())

    for c in range(C):
        pack(c)

    for copy in ins:
        copy.wait()

    total_rows = 2 * nz * msg

    def fill_weights():
        for n, ref in enumerate((w_gate, w_up)):
            wt[n * hidden : (n + 1) * hidden, :] = ref[...].T

    def fill_activation():
        def body(i):
            gv = s_gate[i].astype(F32)
            act[i] = (gv * jax.nn.sigmoid(gv) * s_up[i].astype(F32)).astype(BF)

        loop(0, 2 * nz, body)

    def turn(ref, lo):
        for m in range(ref.shape[2] // 128):
            at = lo + m * 128
            xt[at : at + 128, :] = ref[:, :, m * 128 : (m + 1) * 128].reshape(total_rows, 128).T

    def fill_down():
        turn(x1, 0)
        o_down[...] = dot_nn(xt[0:feats, :], act[...].reshape(total_rows, hidden)).astype(BF)

    def fill_second():
        for i in range(2):
            @pl.when(2 * h + i != y)
            def _():
                y_copy(3, 0, i).wait_recv()

        for i in range(2):
            pack_c[i * toks : (i + 1) * toks, :] = r_tok[i, lead:feats].T

    def picks(c):
        g = lax.rem(zq + c, C)
        ids = lax.broadcasted_iota(jnp.int32, (G * msg, toks), 0).astype(F32) + (g * (G * msg)).astype(F32)
        both = [((targets[i] == ids).astype(F32) + (targets[2 + i] == ids).astype(F32)).astype(BF) for i in range(2)]
        return g, jnp.concatenate(both, axis=1)

    def send_second(c):
        g, one_hot = picks(c)
        sb2[pl.ds(g * G, G)] = dot_nn(one_hot, pack_c[...]).astype(BF).reshape(G, msg, 2 * feats - w1)
        if c == 0:
            x2[2 * z + h] = sb2[z]
            f2_copy(0, 0).start()
        loop(first(c), G, lambda j: z2_copy(c, j).start())

    def x_copy(c, j):
        k = c * (units - 1) + j - 1
        return remote(pb.at[c, lax.rem(me + j, units)], rx.at[c, j - 1], sem_xs.at[k], sem_xr.at[k], e, dp_to(j))

    def h_copy(c):
        return remote(wb.at[c], rz.at[c], sem_hs.at[c], sem_hr.at[c], e, zh_to)

    def g_copy(c, j):
        k = c * (units - 1) + j - 1
        return remote(hid.at[c, me], hid.at[c, me], sem_gs.at[k], sem_gr.at[k], e, dp_to(j))

    def p_copy(c):
        g = group(c)
        return remote(bg.at[1 - h, pl.ds(g * G, G)], rp.at[pl.ds(g * G, G)], sem_ps.at[c], sem_pr.at[c], pair, d)

    def r_copy(c, j):
        to = recv_z(c, j)
        return remote(ps.at[to], rr.at[z], sem_rs.at[c * G + j], sem_rr.at[c * G + j], to * Y + y, d)

    def t_copy(c, j):
        to = recv_z(c, j)
        return remote(pt.at[to], rt.at[z], sem_ts.at[c * G + j], sem_tr.at[c * G + j], to * Y + y, d)

    def stage_forward(c):
        def body(j):
            z1_copy(c, j).wait_recv()
            f1_copy(c, j).start()

        loop(first(c), G, body)

    def stage_product(c):
        loop(0, G, lambda j: f1_copy(c, j).wait_recv())
        g = group(c)
        left = x1[pl.ds(2 * G * g, 2 * G)].reshape(rows, w1)
        part = dot_nn(left, wd[...]).reshape(units, rows // units, hidden)
        p32[c] = part
        pb[c] = part.astype(BF)
        loop(1, units, lambda j: x_copy(c, j).start())

    def stage_sum(c):
        loop(1, units, lambda j: x_copy(c, j).wait_recv())
        total = p32[c, me]
        for j in range(1, units):
            total = total + rx[c, j - 1].astype(F32)
        w32[c] = total
        if nzh == 2:
            wb[c] = total.astype(BF)
            h_copy(c).start()

    def stage_zh(c):
        total = w32[c]
        if nzh == 2:
            h_copy(c).wait_recv()
            total = total + rz[c].astype(F32)
        hid[c, me] = total.astype(BF)
        loop(1, units, lambda j: g_copy(c, j).start())

    def stage_hidden(c):
        loop(1, units, lambda j: g_copy(c, j).wait_recv())
        g = group(c)
        at = pl.ds(2 * G * g, 2 * G)
        back = hid[c].astype(F32).reshape(rows, hidden)
        gv = s_gate[at].astype(F32).reshape(rows, hidden)
        uv = s_up[at].astype(F32).reshape(rows, hidden)
        sig = jax.nn.sigmoid(gv)
        g_grad = (back * uv * sig * (1.0 + gv * (1.0 - sig))).astype(BF)
        u_grad = (back * gv * sig).astype(BF)
        joined = jnp.concatenate([g_grad, u_grad], axis=1)
        gg[at] = g_grad.reshape(2 * G, msg, hidden)
        ug[at] = u_grad.reshape(2 * G, msg, hidden)
        block = dot_nn(joined, wt[...]).astype(BF).reshape(G, 2, msg, feats)
        bg[0, pl.ds(g * G, G)] = block[:, 0]
        bg[1, pl.ds(g * G, G)] = block[:, 1]
        p_copy(c).start()

    def stage_pair(c):
        p_copy(c).wait_recv()
        at = pl.ds(group(c) * G, G)
        total = (bg[h, at].astype(F32) + rp[at].astype(F32)).astype(BF)
        ps[at] = total[:, :, 0:wide]
        tail = total[:, :, wide:]
        below = jnp.concatenate([tail[:, half:], jnp.zeros((G, 2 * half - msg, feats - wide), BF)], axis=1)
        pt[at] = jnp.concatenate([tail[:, 0:half], below], axis=2)
        if c == 0:
            rr[z] = ps[z]
            rt[z] = pt[z]
        loop(first(c), G, lambda j: (r_copy(c, j).start(), t_copy(c, j).start()))

    def stage_gap(c):
        pass

    def fill_both():
        for c in reversed(range(C)):
            send_second(c)
        fill_down()

    stages = [stage_forward, stage_product, stage_sum, stage_gap, stage_zh, stage_hidden, stage_pair]
    fillers = {0: fill_second, 1: fill_weights, 2: fill_activation, C + 1: fill_both}
    for step in range(C + len(stages) - 1):
        for s in reversed(range(len(stages))):
            c = step - s
            if 0 <= c < C:
                stages[s](c)
        if step in fillers:
            fillers[step]()

    for c in range(C):
        def forward2(j):
            z2_copy(c, j).wait_recv()
            f2_copy(c, j).start()

        loop(first(c), G, forward2)

    for c in range(C):
        loop(0, G, lambda j: f2_copy(c, j).wait_recv())
    turn(x2, w1)
    for grads, out in ((gg, o_gate), (ug, o_up)):
        out[...] = dot_nn(xt[feats : 2 * feats, :], grads[...].reshape(total_rows, hidden)).astype(BF)

    for c in range(C):
        loop(first(c), G, lambda j: (r_copy(c, j).wait_recv(), t_copy(c, j).wait_recv()))
        g, one_hot = picks(c)
        part = dot_tn(rr[pl.ds(g * G, G)].reshape(G * msg, wide), one_hot)
        split = one_hot.reshape(G, msg, 2 * toks)
        tails = rt[pl.ds(g * G, G)].reshape(G * half, 128)
        above = split[:, 0:half].reshape(G * half, 2 * toks)
        below = jnp.concatenate([split[:, half:], jnp.zeros((G, 2 * half - msg, 2 * toks), BF)], axis=1)
        left = dot_tn(tails, above)[0:64] + dot_tn(tails, below.reshape(G * half, 2 * toks))[64:]
        if c == 0:
            out32[0:wide] = part
            out32[wide:] = left
        else:
            out32[0:wide] += part
            out32[wide:] += left

    def o_copy(i, j):
        return remote(ot.at[i], ro.at[par], sem_os.at[i], sem_or.at[j], z * Y + 2 * h + i, d)

    for i in range(2):
        ot[i] = out32[:, i * toks : (i + 1) * toks].astype(BF)
        s = 2 * h + i

        for p in range(2):
            @pl.when((s != y) & (par == p))
            def _():
                o_copy(i, p).start()

        @pl.when(s == y)
        def _():
            ro[par] = ot[i]

    for j in range(2):
        @pl.when(y // 2 + 2 * j != y)
        def _():
            o_copy(0, j).wait_recv()

    o_tok[...] = (ro[0].astype(F32) + ro[1].astype(F32)).astype(BF)

    for j in range(2):
        @pl.when(y // 2 + 2 * j != y)
        def _():
            for kind in range(4):
                y_copy(kind, j, h).wait_send()

    for c in range(C):
        def sent(j):
            z1_copy(c, j).wait_send()
            z2_copy(c, j).wait_send()
            r_copy(c, j).wait_send()
            t_copy(c, j).wait_send()

        loop(first(c), G, sent)

        def forwarded(j):
            f1_copy(c, j).wait_send()
            f2_copy(c, j).wait_send()

        loop(0, G, forwarded)
        loop(1, units, lambda j: (x_copy(c, j).wait_send(), g_copy(c, j).wait_send()))
        if nzh == 2:
            h_copy(c).wait_send()
        p_copy(c).wait_send()
    for i in range(2):
        @pl.when(2 * h + i != y)
        def _():
            o_copy(i, 0).wait_send()


def shards(dp_shape, chunks, tokens_in, grad_out, routes, gate_probs, saved_gate, saved_up, w_gate, w_up, w_down):
    groups = lax.axis_size("expert")
    nx, nzh = dp_shape
    nz = groups // Y
    slot_rows, hidden = saved_gate.shape[1:]
    cap = slot_rows // groups
    toks, feats = tokens_in.shape
    msg = 2 * cap
    C = chunks
    G = nz // C
    w1 = -(-feats // 128) * 128
    w2 = 2 * feats - w1
    wide, half = feats - 64, -(-msg // 16) * 8
    units = 2 * nx
    unit = 2 * G * msg // units
    dma = lambda n: pltpu.SemaphoreType.DMA((n,))
    vm = lambda shape, dtype=BF: pltpu.VMEM(shape, dtype)
    scratch = [
        vm((2 * nz, msg, hidden)), vm((2 * nz, msg, hidden)), vm((feats, hidden)), vm((feats, hidden)), dma(5),
        vm((8, toks), F32), vm((2, feats, toks)), vm((2, feats, toks)), vm((2, 8, toks), F32),
        vm((4 * toks, w1)), vm((2 * toks, w2)),
        vm((nz, msg, w1)), vm((nz, msg, w2)), vm((2 * nz, msg, w1)), vm((2 * nz, msg, w2)),
        vm((w1, hidden)), vm((2 * nz, msg, hidden)),
        vm((C, units, unit, hidden), F32), vm((C, units, unit, hidden)), vm((C, units - 1, unit, hidden)),
        vm((C, unit, hidden), F32), vm((C, unit, hidden)), vm((C, unit, hidden)),
        vm((C, units, unit, hidden)),
        vm((2 * feats, 2 * nz * msg)), vm((2 * hidden, feats)), vm((feats, 2 * toks), F32),
        vm((2 * nz, msg, hidden)), vm((2 * nz, msg, hidden)),
        vm((2, nz, msg, feats)), vm((nz, msg, feats)),
        vm((nz, msg, wide)), vm((nz, half, 128)), vm((nz, msg, wide)), vm((nz, half, 128)),
        vm((2, feats, toks)), vm((2, feats, toks)),
        dma(8), dma(8), dma(nz), dma(nz), dma(nz), dma(nz), dma(nz), dma(nz), dma(nz), dma(nz),
        dma(C * (units - 1)), dma(C * (units - 1)), dma(C), dma(C), dma(C * (units - 1)), dma(C * (units - 1)),
        dma(C), dma(C), dma(nz), dma(nz), dma(nz), dma(nz), dma(2), dma(2),
    ]
    o_tok, o_gate, o_up, o_down = pl.pallas_call(
        functools.partial(kernel, (nz, nx, nzh, cap, C)),
        out_shape=(
            jax.ShapeDtypeStruct((feats, toks), BF),
            jax.ShapeDtypeStruct((feats, hidden), BF),
            jax.ShapeDtypeStruct((feats, hidden), BF),
            jax.ShapeDtypeStruct((feats, hidden), BF),
        ),
        in_specs=[pl.BlockSpec(memory_space=pltpu.VMEM)] * 4 + [pl.BlockSpec(memory_space=pltpu.HBM)] * 5,
        out_specs=(pl.BlockSpec(memory_space=pltpu.VMEM),) * 4,
        scratch_shapes=scratch,
        compiler_params=pltpu.CompilerParams(
            collective_id=0, has_side_effects=True, vmem_limit_bytes=60 * 1024 * 1024
        ),
    )(
        tokens_in.T, grad_out.T, routes.T, gate_probs.T,
        saved_gate.reshape(2 * nz, msg, hidden), saved_up.reshape(2 * nz, msg, hidden),
        w_gate[0], w_up[0], w_down[0].T,
    )
    return o_tok.T, o_gate[None], o_up[None], o_down.T[None]


def build(mesh, dp_shape, chunks):
    return jax.shard_map(
        functools.partial(shards, dp_shape, chunks),
        mesh=mesh,
        in_specs=(
            P("expert", "dp"),
            P("expert", "dp"),
            P("expert", None),
            P("expert", None),
            P("expert", None, None),
            P("expert", None, None),
            P("expert", "dp", None),
            P("expert", "dp", None),
            P("expert", None, "dp"),
        ),
        out_specs=(
            P("expert", "dp"),
            P("expert", "dp", None),
            P("expert", "dp", None),
            P("expert", None, "dp"),
        ),
        check_vma=False,
    )


def solution(mesh):
    return build(mesh, (4, 2), CHUNKS)
```

```python
import functools

import jax
import jax.numpy as jnp
from jax import lax
from jax.experimental import pallas as pl
from jax.experimental.pallas import tpu as pltpu
from jax.sharding import PartitionSpec as P

MESH = pl.DeviceIdType.MESH
Y = 4
CHUNKS = 2
BF = jnp.bfloat16
F32 = jnp.float32


def dot_nn(a, b):
    return lax.dot_general(a, b, (((1,), (0,)), ((), ())), preferred_element_type=F32)


def dot_nt(a, b):
    return lax.dot_general(a, b, (((1,), (1,)), ((), ())), preferred_element_type=F32)


def dot_tn(a, b):
    return lax.dot_general(a, b, (((0,), (0,)), ((), ())), preferred_element_type=F32)


def kernel(
    cfg,
    tok_t, grad_t, routes_t, probs_t, h_gate, h_up, h_wg, h_wu, h_wd,
    o_tok, o_gate, o_up, o_down,
    s_gate, s_up, w_gate, w_up, sem_in,
    meta, r_tok, r_grad, r_meta, pack_b, pack_c,
    sb1, sb2, x1, x2, wd, act,
    p32, pb, rx, w32, wb, rz, hid,
    xt, wt, out32, gg, ug, bg, rp, ps, pt, rr, rt, ot, ro,
    sem_ys, sem_yr, sem_z1s, sem_z1r, sem_f1s, sem_f1r, sem_z2s, sem_z2r, sem_f2s, sem_f2r,
    sem_xs, sem_xr, sem_hs, sem_hr, sem_gs, sem_gr,
    sem_ps, sem_pr, sem_rs, sem_rr, sem_ts, sem_tr, sem_os, sem_or,
):
    nz, nx, nzh, cap, C = cfg
    G = nz // C
    feats, toks = tok_t.shape
    hidden = h_gate.shape[2]
    w1 = sb1.shape[2]
    msg = 2 * cap
    units = 2 * nx
    rows = 2 * G * msg
    wide, half = ps.shape[2], pt.shape[1]

    e = lax.axis_index("expert")
    d = lax.axis_index("dp")
    y, z = lax.rem(e, Y), lax.div(e, Y)
    core, zh, x = lax.rem(d, 2), lax.rem(lax.div(d, 2), nzh), lax.div(d, 2 * nzh)
    par, h = lax.div(y, 2), lax.rem(y, 2)
    zq, zr = lax.div(z, G), lax.rem(z, G)
    pair = z * Y + (y + 1 - 2 * h)
    me = core * nx + x
    zh_to = (x * nzh + (1 - zh)) * 2 + core

    def dp_to(j):
        v = lax.rem(me + j, units)
        return (lax.rem(v, nx) * nzh + zh) * 2 + lax.div(v, nx)

    def send_z(c, j):
        return lax.rem(zq + c, C) * G + lax.rem(zr + j, G)

    def recv_z(c, j):
        return lax.rem(zq + (C - c), C) * G + lax.rem(zr + G - j, G)

    def group(c):
        return lax.rem(zq + (C - c), C)

    def remote(src, dst, ss, rs, ee, dd):
        return pltpu.make_async_remote_copy(
            src_ref=src, dst_ref=dst, send_sem=ss, recv_sem=rs,
            device_id=(ee, dd), device_id_type=MESH,
        )

    def loop(lo, hi, body):
        if hi - lo == 1:
            body(lo)
        elif hi > lo:
            lax.fori_loop(lo, hi, lambda i, _: (body(i), 0)[1], 0)

    ins = [
        pltpu.make_async_copy(src, dst, sem_in.at[n])
        for n, (src, dst) in enumerate(
            ((h_gate, s_gate), (h_up, s_up), (h_wd, wd.at[0:feats]), (h_wg, w_gate), (h_wu, w_up))
        )
    ]
    for copy in ins:
        copy.start()
    wd[feats:, :] = jnp.zeros((w1 - feats, hidden), BF)

    barrier = pltpu.get_barrier_semaphore()

    def greet(ee, dd):
        pl.semaphore_signal(barrier, inc=1, device_id=(ee, dd), device_id_type=MESH)

    for j in range(1, Y):
        greet(z * Y + (y + j) % Y, d)
    loop(1, nz, lambda j: greet(lax.rem(z + j, nz) * Y + y, d))
    loop(1, units, lambda j: greet(e, dp_to(j)))
    if nzh == 2:
        greet(e, zh_to)

    r0, r1 = routes_t[0:1, :], routes_t[1:2, :]
    eid = lax.broadcasted_iota(jnp.int32, (2 * nz, toks), 0)
    hit0, hit1 = (r0 == eid).astype(F32), (r1 == eid).astype(F32)
    upper = (
        lax.broadcasted_iota(jnp.int32, (toks, toks), 0) < lax.broadcasted_iota(jnp.int32, (toks, toks), 1)
    ).astype(BF)
    before = dot_nn((hit0 + hit1).astype(BF), upper)
    for k, (r, hit) in enumerate(((r0, hit0), (r1, hit1))):
        slot = jnp.sum(before * hit, axis=0, keepdims=True)
        meta[k : k + 1, :] = slot + ((r // 2) * msg).astype(F32)
        meta[2 + k : 3 + k, :] = (r % 2).astype(F32)
        meta[4 + k : 5 + k, :] = probs_t[k : k + 1, :]
    meta[6:8, :] = jnp.zeros((2, toks), F32)

    pl.semaphore_wait(barrier, (Y - 1) + (nz - 1) + (units - 1) + (1 if nzh == 2 else 0))

    lead = w1 - feats
    sets = (
        (grad_t, lambda i: r_grad.at[i]),
        (meta, lambda i: r_meta.at[i]),
        (tok_t.at[0:lead], lambda i: r_tok.at[i, 0:lead]),
        (tok_t.at[lead:feats], lambda i: r_tok.at[i, lead:feats]),
    )

    def y_copy(kind, j, i):
        src, dst = sets[kind]
        return remote(src, dst(i), sem_ys.at[kind * 2 + j], sem_yr.at[kind * 2 + i], z * Y + y // 2 + 2 * j, d)

    for j in range(2):
        to = y // 2 + 2 * j

        @pl.when(to != y)
        def _():
            for kind in range(4):
                y_copy(kind, j, h).start()

        @pl.when(to == y)
        def _():
            r_grad[h] = grad_t[...]
            r_meta[h] = meta[...]
            r_tok[h] = tok_t[...]

    for i in range(2):
        @pl.when(2 * h + i != y)
        def _():
            for kind in range(3):
                y_copy(kind, 0, i).wait_recv()

    targets = []
    parity = par.astype(F32)
    for k in range(2):
        for i in range(2):
            t = r_meta[i, k : k + 1, :] + float(cap * i)
            targets.append(jnp.where(r_meta[i, 2 + k : 3 + k, :] == parity, t, -1.0))
            lanes = pl.ds((2 * k + i) * toks, toks)
            scaled = r_grad[i].astype(F32) * r_meta[i, 4 + k : 5 + k, :]
            both = jnp.concatenate([scaled.astype(BF), r_tok[i, 0:lead]], axis=0)
            pack_b[lanes, :] = both.T

    def z1_copy(c, j):
        to = send_z(c, j)
        return remote(sb1.at[to], x1.at[2 * z + h], sem_z1s.at[c * G + j], sem_z1r.at[c * G + j], to * Y + y, d)

    def z2_copy(c, j):
        to = send_z(c, j)
        return remote(sb2.at[to], x2.at[2 * z + h], sem_z2s.at[c * G + j], sem_z2r.at[c * G + j], to * Y + y, d)

    def f1_copy(c, j):
        at = 2 * recv_z(c, j) + h
        return remote(x1.at[at], x1.at[at], sem_f1s.at[c * G + j], sem_f1r.at[c * G + j], pair, d)

    def f2_copy(c, j):
        at = 2 * recv_z(c, j) + h
        return remote(x2.at[at], x2.at[at], sem_f2s.at[c * G + j], sem_f2r.at[c * G + j], pair, d)

    def first(c):
        return 1 if c == 0 else 0

    def pack(c):
        g = lax.rem(zq + c, C)
        base = (g * (G * msg)).astype(F32)
        ids = lax.broadcasted_iota(jnp.int32, (G * msg, toks), 0).astype(F32) + base
        one_hot = jnp.concatenate([(t == ids).astype(BF) for t in targets], axis=1)
        sb1[pl.ds(g * G, G)] = dot_nn(one_hot, pack_b[...]).astype(BF).reshape(G, msg, w1)
        if c == 0:
            x1[2 * z + h] = sb1[z]
            f1_copy(0, 0).start()
        loop(first(c), G, lambda j: z1_copy(c, j).start())

    for c in range(C):
        pack(c)

    for copy in ins:
        copy.wait()

    total_rows = 2 * nz * msg

    def fill_weights():
        for n, ref in enumerate((w_gate, w_up)):
            wt[n * hidden : (n + 1) * hidden, :] = ref[...].T

    def fill_activation():
        def body(i):
            gv = s_gate[i].astype(F32)
            act[i] = (gv * jax.nn.sigmoid(gv) * s_up[i].astype(F32)).astype(BF)

        loop(0, 2 * nz, body)

    def turn(ref, lo):
        for m in range(ref.shape[2] // 128):
            at = lo + m * 128
            xt[at : at + 128, :] = ref[:, :, m * 128 : (m + 1) * 128].reshape(total_rows, 128).T

    def fill_down():
        turn(x1, 0)
        o_down[...] = dot_nn(xt[0:feats, :], act[...].reshape(total_rows, hidden)).astype(BF)

    def fill_second():
        for i in range(2):
            @pl.when(2 * h + i != y)
            def _():
                y_copy(3, 0, i).wait_recv()

        for i in range(2):
            pack_c[i * toks : (i + 1) * toks, :] = r_tok[i, lead:feats].T

    def picks(c):
        g = lax.rem(zq + c, C)
        ids = lax.broadcasted_iota(jnp.int32, (G * msg, toks), 0).astype(F32) + (g * (G * msg)).astype(F32)
        both = [((targets[i] == ids).astype(F32) + (targets[2 + i] == ids).astype(F32)).astype(BF) for i in range(2)]
        return g, jnp.concatenate(both, axis=1)

    def send_second(c):
        g, one_hot = picks(c)
        sb2[pl.ds(g * G, G)] = dot_nn(one_hot, pack_c[...]).astype(BF).reshape(G, msg, 2 * feats - w1)
        if c == 0:
            x2[2 * z + h] = sb2[z]
            f2_copy(0, 0).start()
        loop(first(c), G, lambda j: z2_copy(c, j).start())

    def x_copy(c, j):
        k = c * (units - 1) + j - 1
        return remote(pb.at[c, lax.rem(me + j, units)], rx.at[c, j - 1], sem_xs.at[k], sem_xr.at[k], e, dp_to(j))

    def h_copy(c):
        return remote(wb.at[c], rz.at[c], sem_hs.at[c], sem_hr.at[c], e, zh_to)

    def g_copy(c, j):
        k = c * (units - 1) + j - 1
        return remote(hid.at[c, me], hid.at[c, me], sem_gs.at[k], sem_gr.at[k], e, dp_to(j))

    def p_copy(c):
        g = group(c)
        return remote(bg.at[1 - h, pl.ds(g * G, G)], rp.at[pl.ds(g * G, G)], sem_ps.at[c], sem_pr.at[c], pair, d)

    def r_copy(c, j):
        to = recv_z(c, j)
        return remote(ps.at[to], rr.at[z], sem_rs.at[c * G + j], sem_rr.at[c * G + j], to * Y + y, d)

    def t_copy(c, j):
        to = recv_z(c, j)
        return remote(pt.at[to], rt.at[z], sem_ts.at[c * G + j], sem_tr.at[c * G + j], to * Y + y, d)

    def stage_forward(c):
        def body(j):
            z1_copy(c, j).wait_recv()
            f1_copy(c, j).start()

        loop(first(c), G, body)

    def stage_product(c):
        loop(0, G, lambda j: f1_copy(c, j).wait_recv())
        g = group(c)
        left = x1[pl.ds(2 * G * g, 2 * G)].reshape(rows, w1)
        part = dot_nn(left, wd[...]).reshape(units, rows // units, hidden)
        p32[c] = part
        pb[c] = part.astype(BF)
        loop(1, units, lambda j: x_copy(c, j).start())

    def stage_sum(c):
        loop(1, units, lambda j: x_copy(c, j).wait_recv())
        total = p32[c, me]
        for j in range(1, units):
            total = total + rx[c, j - 1].astype(F32)
        w32[c] = total
        if nzh == 2:
            wb[c] = total.astype(BF)
            h_copy(c).start()

    def stage_zh(c):
        total = w32[c]
        if nzh == 2:
            h_copy(c).wait_recv()
            total = total + rz[c].astype(F32)
        hid[c, me] = total.astype(BF)
        loop(1, units, lambda j: g_copy(c, j).start())

    def stage_hidden(c):
        loop(1, units, lambda j: g_copy(c, j).wait_recv())
        g = group(c)
        at = pl.ds(2 * G * g, 2 * G)
        back = hid[c].astype(F32).reshape(rows, hidden)
        gv = s_gate[at].astype(F32).reshape(rows, hidden)
        uv = s_up[at].astype(F32).reshape(rows, hidden)
        sig = jax.nn.sigmoid(gv)
        g_grad = (back * uv * sig * (1.0 + gv * (1.0 - sig))).astype(BF)
        u_grad = (back * gv * sig).astype(BF)
        joined = jnp.concatenate([g_grad, u_grad], axis=1)
        gg[at] = g_grad.reshape(2 * G, msg, hidden)
        ug[at] = u_grad.reshape(2 * G, msg, hidden)
        block = dot_nn(joined, wt[...]).astype(BF).reshape(G, 2, msg, feats)
        bg[0, pl.ds(g * G, G)] = block[:, 0]
        bg[1, pl.ds(g * G, G)] = block[:, 1]
        p_copy(c).start()

    def stage_pair(c):
        p_copy(c).wait_recv()
        at = pl.ds(group(c) * G, G)
        total = (bg[h, at].astype(F32) + rp[at].astype(F32)).astype(BF)
        ps[at] = total[:, :, 0:wide]
        tail = total[:, :, wide:]
        below = jnp.concatenate([tail[:, half:], jnp.zeros((G, 2 * half - msg, feats - wide), BF)], axis=1)
        pt[at] = jnp.concatenate([tail[:, 0:half], below], axis=2)
        if c == 0:
            rr[z] = ps[z]
            rt[z] = pt[z]
        loop(first(c), G, lambda j: (r_copy(c, j).start(), t_copy(c, j).start()))

    def stage_gap(c):
        pass

    def fill_both():
        for c in reversed(range(C)):
            send_second(c)
        fill_down()

    stages = [stage_forward, stage_product, stage_sum, stage_gap, stage_zh, stage_hidden, stage_pair]
    fillers = {0: fill_second, 1: fill_weights, 2: fill_activation, C + 1: fill_both}
    for step in range(C + len(stages) - 1):
        for s in reversed(range(len(stages))):
            c = step - s
            if 0 <= c < C:
                stages[s](c)
        if step in fillers:
            fillers[step]()

    for c in range(C):
        def forward2(j):
            z2_copy(c, j).wait_recv()
            f2_copy(c, j).start()

        loop(first(c), G, forward2)

    for c in range(C):
        loop(first(c), G, lambda j: (r_copy(c, j).wait_recv(), t_copy(c, j).wait_recv()))
        g, one_hot = picks(c)
        part = dot_tn(rr[pl.ds(g * G, G)].reshape(G * msg, wide), one_hot)
        split = one_hot.reshape(G, msg, 2 * toks)
        tails = rt[pl.ds(g * G, G)].reshape(G * half, 128)
        above = split[:, 0:half].reshape(G * half, 2 * toks)
        below = jnp.concatenate([split[:, half:], jnp.zeros((G, 2 * half - msg, 2 * toks), BF)], axis=1)
        left = dot_tn(tails, above)[0:64] + dot_tn(tails, below.reshape(G * half, 2 * toks))[64:]
        if c == 0:
            out32[0:wide] = part
            out32[wide:] = left
        else:
            out32[0:wide] += part
            out32[wide:] += left

    def o_copy(i, j):
        return remote(ot.at[i], ro.at[par], sem_os.at[i], sem_or.at[j], z * Y + 2 * h + i, d)

    for i in range(2):
        ot[i] = out32[:, i * toks : (i + 1) * toks].astype(BF)
        s = 2 * h + i

        for p in range(2):
            @pl.when((s != y) & (par == p))
            def _():
                o_copy(i, p).start()

        @pl.when(s == y)
        def _():
            ro[par] = ot[i]

    for c in range(C):
        loop(0, G, lambda j: f2_copy(c, j).wait_recv())
    turn(x2, w1)
    for grads, out in ((gg, o_gate), (ug, o_up)):
        out[...] = dot_nn(xt[feats : 2 * feats, :], grads[...].reshape(total_rows, hidden)).astype(BF)

    for j in range(2):
        @pl.when(y // 2 + 2 * j != y)
        def _():
            o_copy(0, j).wait_recv()

    o_tok[...] = (ro[0].astype(F32) + ro[1].astype(F32)).astype(BF)

    for j in range(2):
        @pl.when(y // 2 + 2 * j != y)
        def _():
            for kind in range(4):
                y_copy(kind, j, h).wait_send()

    for c in range(C):
        def sent(j):
            z1_copy(c, j).wait_send()
            z2_copy(c, j).wait_send()
            r_copy(c, j).wait_send()
            t_copy(c, j).wait_send()

        loop(first(c), G, sent)

        def forwarded(j):
            f1_copy(c, j).wait_send()
            f2_copy(c, j).wait_send()

        loop(0, G, forwarded)
        loop(1, units, lambda j: (x_copy(c, j).wait_send(), g_copy(c, j).wait_send()))
        if nzh == 2:
            h_copy(c).wait_send()
        p_copy(c).wait_send()
    for i in range(2):
        @pl.when(2 * h + i != y)
        def _():
            o_copy(i, 0).wait_send()


def shards(dp_shape, chunks, tokens_in, grad_out, routes, gate_probs, saved_gate, saved_up, w_gate, w_up, w_down):
    groups = lax.axis_size("expert")
    nx, nzh = dp_shape
    nz = groups // Y
    slot_rows, hidden = saved_gate.shape[1:]
    cap = slot_rows // groups
    toks, feats = tokens_in.shape
    msg = 2 * cap
    C = chunks
    G = nz // C
    w1 = -(-feats // 128) * 128
    w2 = 2 * feats - w1
    wide, half = feats - 64, -(-msg // 16) * 8
    units = 2 * nx
    unit = 2 * G * msg // units
    dma = lambda n: pltpu.SemaphoreType.DMA((n,))
    vm = lambda shape, dtype=BF: pltpu.VMEM(shape, dtype)
    scratch = [
        vm((2 * nz, msg, hidden)), vm((2 * nz, msg, hidden)), vm((feats, hidden)), vm((feats, hidden)), dma(5),
        vm((8, toks), F32), vm((2, feats, toks)), vm((2, feats, toks)), vm((2, 8, toks), F32),
        vm((4 * toks, w1)), vm((2 * toks, w2)),
        vm((nz, msg, w1)), vm((nz, msg, w2)), vm((2 * nz, msg, w1)), vm((2 * nz, msg, w2)),
        vm((w1, hidden)), vm((2 * nz, msg, hidden)),
        vm((C, units, unit, hidden), F32), vm((C, units, unit, hidden)), vm((C, units - 1, unit, hidden)),
        vm((C, unit, hidden), F32), vm((C, unit, hidden)), vm((C, unit, hidden)),
        vm((C, units, unit, hidden)),
        vm((2 * feats, 2 * nz * msg)), vm((2 * hidden, feats)), vm((feats, 2 * toks), F32),
        vm((2 * nz, msg, hidden)), vm((2 * nz, msg, hidden)),
        vm((2, nz, msg, feats)), vm((nz, msg, feats)),
        vm((nz, msg, wide)), vm((nz, half, 128)), vm((nz, msg, wide)), vm((nz, half, 128)),
        vm((2, feats, toks)), vm((2, feats, toks)),
        dma(8), dma(8), dma(nz), dma(nz), dma(nz), dma(nz), dma(nz), dma(nz), dma(nz), dma(nz),
        dma(C * (units - 1)), dma(C * (units - 1)), dma(C), dma(C), dma(C * (units - 1)), dma(C * (units - 1)),
        dma(C), dma(C), dma(nz), dma(nz), dma(nz), dma(nz), dma(2), dma(2),
    ]
    o_tok, o_gate, o_up, o_down = pl.pallas_call(
        functools.partial(kernel, (nz, nx, nzh, cap, C)),
        out_shape=(
            jax.ShapeDtypeStruct((feats, toks), BF),
            jax.ShapeDtypeStruct((feats, hidden), BF),
            jax.ShapeDtypeStruct((feats, hidden), BF),
            jax.ShapeDtypeStruct((feats, hidden), BF),
        ),
        in_specs=[pl.BlockSpec(memory_space=pltpu.VMEM)] * 4 + [pl.BlockSpec(memory_space=pltpu.HBM)] * 5,
        out_specs=(pl.BlockSpec(memory_space=pltpu.VMEM),) * 4,
        scratch_shapes=scratch,
        compiler_params=pltpu.CompilerParams(
            collective_id=0, has_side_effects=True, vmem_limit_bytes=60 * 1024 * 1024
        ),
    )(
        tokens_in.T, grad_out.T, routes.T, gate_probs.T,
        saved_gate.reshape(2 * nz, msg, hidden), saved_up.reshape(2 * nz, msg, hidden),
        w_gate[0], w_up[0], w_down[0].T,
    )
    return o_tok.T, o_gate[None], o_up[None], o_down.T[None]


def build(mesh, dp_shape, chunks):
    return jax.shard_map(
        functools.partial(shards, dp_shape, chunks),
        mesh=mesh,
        in_specs=(
            P("expert", "dp"),
            P("expert", "dp"),
            P("expert", None),
            P("expert", None),
            P("expert", None, None),
            P("expert", None, None),
            P("expert", "dp", None),
            P("expert", "dp", None),
            P("expert", None, "dp"),
        ),
        out_specs=(
            P("expert", "dp"),
            P("expert", "dp", None),
            P("expert", "dp", None),
            P("expert", None, "dp"),
        ),
        check_vma=False,
    )


def solution(mesh):
    return build(mesh, (4, 2), CHUNKS)
```
